32 devices in a mesh: tm: 16 (over z, x, core), space: 2 (over y).
Axes of the slice: x: 2, y: 2, z: 4, core: 2. Of those that a mesh axis runs over, the one named last changes fastest.
Arguments:
- rhs: float32 [16, 3, 128, 256], P('tm', None, 'space'), may hold values from -6 to 6
- depth: float32 [128, 256], P('space'), may hold values from 0.25 to 2
- coriolis: float32 [128, 256], P('space'), may hold values from -0.05 to 0.05
Outputs:
- preconditioned: float32 [16, 3, 128, 256], P('tm', None, 'space')
The draws below stay inside these ranges and needn't reach their ends.
All inputs are finite; a program needn't handle non-finite values.
Results may differ from the reference program's by a relative error of at most 0.0003.
Values sent between devices are 32-bit elements; how exact they have to be, the bound alone decides.
A program may use at most 64 MiB of HBM per device.

```python
import math
import jax
import jax.numpy as jnp
from jax import lax

NY = 256
SWEEPS = 8
STEPS = 16
NX = 128


def block_scale(stream_key, shape, pieces, smallest, largest):
    def one(dim, parts):
        draws = jax.random.uniform(jax.random.fold_in(jax.random.fold_in(stream_key, 6), dim), (parts,), jnp.float32, smallest / len(pieces), largest / len(pieces))
        return jnp.repeat(jnp.exp(draws), shape[dim] // parts).reshape((-1,) + (1,) * (len(shape) - dim - 1))

    factor_of = one(*pieces[0])
    for cut in pieces[1:]:
        factor_of = factor_of * one(*cut)
    return factor_of


def noise(stream_key, extent, scale, reach, shards=(), kind=jnp.bfloat16):
    drawn = jax.random.normal(stream_key, extent, jnp.float32) * scale
    if len(shards) > 0:
        drawn = block_scale(stream_key, extent, shards, -0.22, 0.18) * drawn
    return jnp.clip(drawn, min=-reach, max=reach).astype(kind)


def setup_inputs(seed: int = 0) -> dict:
    keys = jax.random.split(jax.random.key(seed), 4)
    rhs = noise(keys[0], (STEPS, 3, NX, NY), 1.0, 6.0, ((0, 16), (2, 2)), jnp.float32)
    depth = jnp.clip(jnp.exp(math.log(2.0) - 2.0794415 * jax.random.uniform(keys[1], (NX, NY), jnp.float32) ** block_scale(keys[1], (NX, NY), ((0, 2),), -0.2, 0.2)), 0.25, 2.0)
    coriolis = jnp.clip(jax.random.uniform(keys[2], (NX, NY), jnp.float32, -0.05, 0.05) * block_scale(keys[2], (NX, NY), ((0, 2),), -0.4, 0.0), -0.05, 0.05)
    return {"rhs": rhs, "depth": depth, "coriolis": coriolis}


RHO = 0.9
SIGMA = 0.01


def pad_rows(field):
    return jnp.pad(field, ((1, 1), (0, 0)))


def tendency(height, east, north, height_ext, east_ext, depth, coriolis):
    height_dx = height_ext[2:] - height_ext[:-2]
    east_dx = east_ext[2:] - east_ext[:-2]
    height_dy = jnp.roll(height, -1, axis=1) - jnp.roll(height, 1, axis=1)
    north_dy = jnp.roll(north, -1, axis=1) - jnp.roll(north, 1, axis=1)
    return jnp.stack([-SIGMA * depth * (east_dx + north_dy),
                      -SIGMA * height_dx + coriolis * north,
                      -SIGMA * height_dy - coriolis * east])


def divide(real_part, imag_part, shift_re, shift_im):
    denom = shift_re * shift_re + shift_im * shift_im
    return ((real_part * shift_re + imag_part * shift_im) / denom,
            (imag_part * shift_re - real_part * shift_im) / denom)


def apply_op(field, depth, coriolis):
    return tendency(field[0], field[1], field[2], pad_rows(field[0]), pad_rows(field[1]), depth, coriolis)


def reference(rhs, depth, coriolis):
    index = jnp.arange(STEPS, dtype=jnp.int32)
    times = index.astype(jnp.float32)
    scale = jnp.power(jnp.float32(RHO), times)
    scaled = rhs * scale[:, None, None, None]
    product = (index[:, None] * index[None, :]) % STEPS
    table_angle = 2.0 * math.pi * product.astype(jnp.float32) / STEPS
    cos_table = jnp.cos(table_angle)
    sin_table = jnp.sin(table_angle)
    hi = lax.Precision.HIGHEST
    spec_re = jnp.einsum("kj,jfxy->kfxy", cos_table, scaled, precision=hi)
    spec_im = -jnp.einsum("kj,jfxy->kfxy", sin_table, scaled, precision=hi)
    theta = 2.0 * math.pi * times / STEPS
    shift_re = 1.0 - RHO * jnp.cos(theta)
    shift_im = RHO * jnp.sin(theta)

    def solve(items):
        right_re, right_im, lam_re, lam_im = items
        work_re, work_im = divide(right_re, right_im, lam_re, lam_im)
        for sweep in range(SWEEPS):
            moved_re = apply_op(work_re, depth, coriolis)
            moved_im = apply_op(work_im, depth, coriolis)
            work_re, work_im = divide(right_re + moved_re, right_im + moved_im, lam_re, lam_im)
        return work_re, work_im

    solved_re, solved_im = lax.map(solve, (spec_re, spec_im, shift_re, shift_im))
    back = (jnp.einsum("jk,kfxy->jfxy", cos_table, solved_re, precision=hi)
            - jnp.einsum("jk,kfxy->jfxy", sin_table, solved_im, precision=hi)) / STEPS
    unscale = jnp.power(jnp.float32(RHO), -times)
    return back * unscale[:, None, None, None]
```

```python
import functools

import jax
import jax.numpy as jnp
import numpy as np
from jax import lax
from jax.experimental import pallas as pl
from jax.experimental.pallas import tpu as pltpu
from jax.sharding import PartitionSpec as P

SWEEPS = 8
RHO = 0.9
SIGMA = 0.01
TERMS = SWEEPS + 1
HALO = 8
MESH = pl.DeviceIdType.MESH


def coefficients(window):
    k = np.arange(window)
    lam = 1.0 - RHO * np.exp(-2j * np.pi * k / window)
    gap = np.arange(-(window - 1), window)
    phase = np.exp(2j * np.pi * gap[:, None] * k[None, :] / window)
    powers = np.stack([lam ** -(n + 1.0) for n in range(TERMS)])
    table = (powers @ phase.T).real / window * RHO ** (-gap.astype(np.float64))
    return table.astype(np.float32)


def gather_kernel(window, rows, coef, rhs, depth, coriolis, out, main, halo, plane, z_acc, send_main, recv_main,
                  send_halo, recv_halo, send_y, recv_y):
    tm, y = lax.axis_index("tm"), lax.axis_index("space")
    z, x, c = tm // 4, tm % 4 // 2, tm % 2
    end = (z == 0) | (z == 3)
    pair = z + 1 - 2 * (z % 2)
    third = jnp.where(z < 2, 2, 1)
    fourth = jnp.where(z < 2, 3, 0)
    order = [z, pair, third, fourth]
    x_other, c_other = z * 4 + (1 - x) * 2 + c, z * 4 + x * 2 + 1 - c

    barrier = pltpu.get_barrier_semaphore()
    for peer in (x_other, c_other):
        pl.semaphore_signal(barrier, inc=1, device_id={"tm": peer}, device_id_type=MESH)
    pl.semaphore_signal(barrier, inc=1, device_id={"space": 1 - y}, device_id_type=MESH)

    @pl.when(z > 0)
    def _():
        pl.semaphore_signal(barrier, inc=1, device_id={"tm": tm - 4}, device_id_type=MESH)

    @pl.when(z < 3)
    def _():
        pl.semaphore_signal(barrier, inc=1, device_id={"tm": tm + 4}, device_id_type=MESH)

    main[tm] = rhs[0]
    plane[0, :rows] = -SIGMA * depth[...]
    plane[1, :rows] = coriolis[...]
    pl.semaphore_wait(barrier, jnp.where(end, 4, 5))

    kinds = ((main, send_main, recv_main), (halo, send_halo, recv_halo))
    pending = []

    def copy(kind, block, slot, peer):
        buf, send, recv = kinds[kind]
        return pltpu.make_async_remote_copy(
            src_ref=buf.at[block], dst_ref=buf.at[block], send_sem=send.at[slot], recv_sem=recv.at[block],
            device_id={"tm": peer}, device_id_type=MESH)

    slots = [0, 0]

    def send(kind, block, peer, when=None):
        slot = slots[kind]
        slots[kind] += 1
        def start():
            copy(kind, block, slot, peer).start()
        def finish():
            copy(kind, block, slot, peer).wait_send()
        if when is None:
            start()
            pending.append(finish)
        else:
            pl.when(when)(start)
            pending.append(lambda: pl.when(when)(finish))

    def arrived(kind, block):
        copy(kind, block, 0, c_other).wait_recv()

    def block_of(zz, same_x, same_c):
        return zz * 4 + (x if same_x else 1 - x) * 2 + (c if same_c else 1 - c)

    edge = pl.multiple_of((1 - y) * (rows - HALO), HALO)
    edges = pltpu.make_async_remote_copy(
        src_ref=main.at[tm, :, pl.ds(edge, HALO), :], dst_ref=halo.at[tm], send_sem=send_y.at[0],
        recv_sem=recv_halo.at[tm], device_id={"space": 1 - y}, device_id_type=MESH)
    fixed = pltpu.make_async_remote_copy(
        src_ref=plane.at[:, pl.ds(edge, HALO), :], dst_ref=plane.at[:, pl.ds(rows, HALO), :], send_sem=send_y.at[1],
        recv_sem=recv_y.at[0], device_id={"space": 1 - y}, device_id_type=MESH)
    edges.start()

    def send_own(kind):
        send(kind, tm, tm + 4, z < 3)
        send(kind, tm, tm - 4, z > 0)
        send(kind, tm, x_other)
        send(kind, tm, c_other)

    def relay_z(kind, stage):
        zz = order[stage]
        block = block_of(zz, True, True)
        arrived(kind, block)
        onward = jnp.where(zz < z, z + 1, z - 1)
        if stage > 0:
            send(kind, block, onward * 4 + x * 2 + c, (onward >= 0) & (onward <= 3))
        send(kind, block, x_other, (end & (c == 1)) if stage == 1 else None)
        send(kind, block, c_other)

    def relay_x(kind, stage):
        block = block_of(order[stage], False, True)
        arrived(kind, block)
        if stage == 0:
            send(kind, block, pair * 4 + x * 2 + c, end | (c == 0))
        send(kind, block, c_other)

    def accumulate(stage):
        blocks = [order[stage] * 4 + q for q in range(4)]
        weights = [[coef[n, tm - b + window - 1] for b in blocks] for n in range(TERMS)]
        step = 32

        def add(parts, n, field, lo, size):
            total = parts[0] * weights[n][0]
            for q in range(1, 4):
                total = total + parts[q] * weights[n][q]
            if stage > 0:
                total = total + z_acc[n, field, lo:lo + size]
            z_acc[n, field, lo:lo + size] = total

        def body(field, carry):
            for lo in range(0, rows, step):
                parts = [main[b, field, lo:lo + step] for b in blocks]
                for n in range(TERMS):
                    add(parts, n, field, lo, step)
            parts = [halo[b, field] for b in blocks]
            for n in range(TERMS):
                add(parts, n, field, rows, HALO)
            return carry

        lax.fori_loop(0, 3, body, 0)

    send_own(0)
    fixed.start()
    edges.wait_recv()
    send_own(1)
    for stage in range(4):
        if stage < 3:
            for kind in (0, 1):
                relay_z(kind, stage + 1)
        for kind in (0, 1):
            relay_x(kind, stage)
        for kind in (0, 1):
            arrived(kind, block_of(order[stage], True, False))
            arrived(kind, block_of(order[stage], False, False))
        accumulate(stage)
    fixed.wait_recv()

    full = rows + HALO
    line = lax.broadcasted_iota(jnp.int32, (full, 256), 0)
    above = jnp.where((line == 0) & (y == 0), 0.0, 1.0)
    below = jnp.where((line == rows - 1) & (y == 1), 0.0, 1.0)

    def dx(a):
        return pltpu.roll(a, full - 1, 0) * below - pltpu.roll(a, 1, 0) * above

    def dy(a):
        return pltpu.roll(a, a.shape[1] - 1, 1) - pltpu.roll(a, 1, 1)

    h, u, v = z_acc[SWEEPS, 0], z_acc[SWEEPS, 1], z_acc[SWEEPS, 2]
    for n in reversed(range(SWEEPS)):
        scaled_depth, turn = plane[0], plane[1]
        h, u, v = (
            z_acc[n, 0] + scaled_depth * (dx(u) + dy(v)),
            z_acc[n, 1] - SIGMA * dx(h) + turn * v,
            z_acc[n, 2] - SIGMA * dy(h) - turn * u,
        )
    out[0, 0] = h[:rows]
    out[0, 1] = u[:rows]
    out[0, 2] = v[:rows]

    for finish in pending:
        finish()
    edges.wait_send()
    fixed.wait_send()


def shards_kernel(rhs, depth, coriolis):
    window = lax.axis_size("tm")
    _, fields, rows, columns = rhs.shape
    vmem = pl.BlockSpec(memory_space=pltpu.VMEM)
    dma = pltpu.SemaphoreType.DMA
    return pl.pallas_call(
        functools.partial(gather_kernel, window, rows),
        out_shape=jax.ShapeDtypeStruct(rhs.shape, jnp.float32),
        in_specs=[pl.BlockSpec(memory_space=pltpu.SMEM), vmem, vmem, vmem],
        out_specs=vmem,
        scratch_shapes=[
            pltpu.VMEM((window, fields, rows, columns), jnp.float32),
            pltpu.VMEM((window, fields, HALO, columns), jnp.float32),
            pltpu.VMEM((2, rows + HALO, columns), jnp.float32),
            pltpu.VMEM((TERMS, fields, rows + HALO, columns), jnp.float32),
            dma((24,)), dma((window,)), dma((24,)), dma((window,)), dma((2,)), dma((1,)),
        ],
        compiler_params=pltpu.CompilerParams(collective_id=0, has_side_effects=True, vmem_limit_bytes=48 << 20),
        cost_estimate=pl.CostEstimate(flops=40_000_000, bytes_accessed=1_000_000, transcendentals=0),
    )(jnp.asarray(coefficients(window)), rhs, depth, coriolis)


def shards_plain(rhs, depth, coriolis):
    window, tiles = lax.axis_size("tm"), lax.axis_size("space")
    tm = lax.axis_index("tm")

    def widen(a, dim):
        length = a.shape[dim]
        last = lax.slice_in_dim(a, length - HALO, length, axis=dim)
        first = lax.slice_in_dim(a, 0, HALO, axis=dim)
        before = lax.ppermute(last, "space", [(i, i + 1) for i in range(tiles - 1)])
        after = lax.ppermute(first, "space", [(i + 1, i) for i in range(tiles - 1)])
        return jnp.concatenate([before, a, after], axis=dim)

    table = jnp.asarray(coefficients(window))
    mine = lax.dynamic_slice_in_dim(table, tm, window, axis=1)[:, ::-1]
    wide = widen(rhs[0], 1)
    everyone = lax.all_gather(wide, "tm")
    sums = jnp.einsum("nj,jfxy->nfxy", mine, everyone, precision=lax.Precision.HIGHEST)
    rows = rhs.shape[2]
    line = lax.axis_index("space") * rows - HALO + jnp.arange(rows + 2 * HALO)
    inside = ((line >= 0) & (line < rows * tiles)).astype(jnp.float32)[:, None]
    deep, turn = -SIGMA * widen(depth, 0), widen(coriolis, 0)

    def dx(a):
        return (jnp.roll(a, -1, 0) - jnp.roll(a, 1, 0)) * inside

    def dy(a):
        return jnp.roll(a, -1, 1) - jnp.roll(a, 1, 1)

    h, u, v = sums[SWEEPS]
    for n in reversed(range(SWEEPS)):
        h, u, v = (sums[n, 0] + deep * (dx(u) + dy(v)), sums[n, 1] - SIGMA * dx(h) + turn * v,
                   sums[n, 2] - SIGMA * dy(h) - turn * u)
    return jnp.stack([h, u, v])[None, :, HALO:rows + HALO]


def solution(mesh):
    in_specs = (P("tm", None, "space", None), P("space", None), P("space", None))
    out_specs = P("tm", None, "space", None)
    body = shards_kernel if (mesh.shape["tm"], mesh.shape["space"]) == (16, 2) else shards_plain
    return jax.shard_map(body, mesh=mesh, in_specs=in_specs, out_specs=out_specs, check_vma=False)
```

```python
import functools

import jax
import jax.numpy as jnp
import numpy as np
from jax import lax
from jax.experimental import pallas as pl
from jax.experimental.pallas import tpu as pltpu
from jax.sharding import PartitionSpec as P

SWEEPS = 8
RHO = 0.9
SIGMA = 0.01
TERMS = SWEEPS + 1
HALO = 8
MESH = pl.DeviceIdType.MESH


def coefficients(window):
    k = np.arange(window)
    lam = 1.0 - RHO * np.exp(-2j * np.pi * k / window)
    gap = np.arange(-(window - 1), window)
    phase = np.exp(2j * np.pi * gap[:, None] * k[None, :] / window)
    powers = np.stack([lam ** -(n + 1.0) for n in range(TERMS)])
    table = (powers @ phase.T).real / window * RHO ** (-gap.astype(np.float64))
    return table.astype(np.float32)


def gather_kernel(window, rows, table, rhs, depth, coriolis, out, main, plane, z_acc, coef, send_sem, send_own, recv_sem,
                  local_sem, send_y, recv_y):
    tm, y = lax.axis_index("tm"), lax.axis_index("space")
    z, x, c = tm // 4, tm % 4 // 2, tm % 2
    end = (z == 0) | (z == 3)
    inner = jnp.logical_not(end)
    fields = range(3)
    pair = z + 1 - 2 * (z % 2)
    order = [z, pair, jnp.where(z < 2, 2, 1), jnp.where(z < 2, 3, 0)]
    x_other, c_other = z * 4 + (1 - x) * 2 + c, z * 4 + x * 2 + 1 - c

    loads = [
        pltpu.make_async_copy(rhs.at[0], main.at[tm, :, pl.ds(0, rows), :], local_sem.at[0]),
        pltpu.make_async_copy(depth, plane.at[0, pl.ds(0, rows), :], local_sem.at[1]),
        pltpu.make_async_copy(coriolis, plane.at[1, pl.ds(0, rows), :], local_sem.at[2]),
    ]
    for load in loads:
        load.start()

    barrier = pltpu.get_barrier_semaphore()
    for peer in (x_other, c_other):
        pl.semaphore_signal(barrier, inc=1, device_id={"tm": peer}, device_id_type=MESH)
    pl.semaphore_signal(barrier, inc=1, device_id={"space": 1 - y}, device_id_type=MESH)

    @pl.when(z > 0)
    def _():
        pl.semaphore_signal(barrier, inc=1, device_id={"tm": tm - 4}, device_id_type=MESH)

    @pl.when(z < 3)
    def _():
        pl.semaphore_signal(barrier, inc=1, device_id={"tm": tm + 4}, device_id_type=MESH)

    for n in range(TERMS):
        for gap in range(2 * window - 1):
            coef[n, gap] = float(table[n, gap])
    for load in loads:
        load.wait()
    pl.semaphore_wait(barrier, jnp.where(end, 4, 5))

    pending = []
    both = lambda *conds: functools.reduce(jnp.logical_and, conds) if conds else None

    def guarded(when, act):
        if when is None:
            act()
        else:
            pl.when(when)(act)

    def copy(block, f, slot, peer):
        return pltpu.make_async_remote_copy(
            src_ref=main.at[block, f], dst_ref=main.at[block, f], send_sem=send_sem.at[slot],
            recv_sem=recv_sem.at[block, f], device_id={"tm": peer}, device_id_type=MESH)

    slots = {}

    def send(key, block, f, peer, start_when=None, finish_when=None):
        fresh = key not in slots
        slot = slots.setdefault(key, len(slots))
        guarded(start_when, lambda: copy(block, f, slot, peer).start())
        if fresh:
            pending.append(lambda: guarded(finish_when, lambda: copy(block, f, slot, peer).wait_send()))

    def arrived(block, f):
        copy(block, f, 0, c_other).wait_recv()

    def block_of(stage, same_x, same_c):
        return order[stage] * 4 + (x if same_x else 1 - x) * 2 + (c if same_c else 1 - c)

    edge = pl.multiple_of((1 - y) * (rows - HALO), HALO)
    tail = pl.ds(rows, HALO)
    edges = pltpu.make_async_remote_copy(
        src_ref=main.at[tm, :, pl.ds(edge, HALO), :], dst_ref=main.at[tm, :, tail, :], send_sem=send_y.at[0],
        recv_sem=recv_y.at[0], device_id={"space": 1 - y}, device_id_type=MESH)
    fixed = pltpu.make_async_remote_copy(
        src_ref=plane.at[:, pl.ds(edge, HALO), :], dst_ref=plane.at[:, tail, :], send_sem=send_y.at[1],
        recv_sem=recv_y.at[1], device_id={"space": 1 - y}, device_id_type=MESH)
    edges.start()

    def own(f, part, index):
        for q, (peer, when) in enumerate([(tm + 4, z < 3), (tm - 4, z > 0), (x_other, None), (c_other, None)]):
            def make(peer=peer, q=q):
                ref = main.at[tm, f, part, :]
                return pltpu.make_async_remote_copy(
                    src_ref=ref, dst_ref=ref, send_sem=send_own.at[index, q], recv_sem=recv_sem.at[tm, f],
                    device_id={"tm": peer}, device_id_type=MESH)
            guarded(when, lambda make=make: make().start())
            pending.append(lambda when=when, make=make: guarded(when, lambda: make().wait_send()))

    def relay_z(stage, f, when=None):
        block = block_of(stage, True, True)
        guarded(when, lambda: arrived(block, f))
        conds = [] if when is None else [when]
        onward = jnp.where(order[stage] < z, z + 1, z - 1)
        send(("z", stage, f), block, f, onward * 4 + x * 2 + c, both(inner, *conds), inner)
        cross = [end & (c == 1)] if stage == 1 else []
        send(("x", stage, f), block, f, x_other, both(*cross, *conds), both(*cross))
        send(("c", stage, f), block, f, c_other, both(*conds))

    def relay_x(stage, f, when=None):
        block = block_of(stage, False, True)
        guarded(when, lambda: arrived(block, f))
        send(("cx", stage, f), block, f, c_other, when)

    def second_route(f, when):
        send(("zx", f), block_of(0, False, True), f, pair * 4 + x * 2 + c, when, end | (c == 0))

    def accumulate(stage, f, first=False):
        arrived(block_of(stage, True, False), f)
        arrived(block_of(stage, False, False), f)
        blocks = [order[stage] * 4 + q for q in range(4)]
        weights = [[coef[n, tm - b + window - 1] for b in blocks] for n in range(TERMS)]
        step = 24

        def body(i, carry):
            part = pl.ds(pl.multiple_of(i * step, 8), step)
            parts = [main[b, f, part] for b in blocks]
            for n in range(TERMS):
                total = parts[0] * weights[n][0]
                for q in range(1, 4):
                    total = total + parts[q] * weights[n][q]
                if not first:
                    total = total + z_acc[n, f, part]
                z_acc[n, f, part] = total
            return carry

        lax.fori_loop(0, (rows + HALO) // step, body, 0)

    body_rows = pl.ds(0, rows)
    own(0, body_rows, 0)
    own(1, body_rows, 1)
    edges.wait_recv()
    own(0, tail, 3)
    own(1, tail, 4)
    own(2, body_rows, 2)
    own(2, tail, 5)
    fixed.start()

    late = end & (c == 0)
    for f in fields:
        relay_z(1, f)
        relay_z(2, f, inner)
        relay_x(0, f)
        second_route(f, end)
    for f in fields:
        relay_z(2, f, end)
        relay_z(3, f, inner)
        relay_x(1, f, jnp.logical_not(late))
        relay_x(2, f, inner)
        accumulate(0, f, first=True)
    for f in fields:
        second_route(f, inner & (c == 0))
    for f in fields:
        relay_z(3, f, end)
        relay_x(2, f, end)
        relay_x(3, f, inner)
    for f in fields:
        relay_x(3, f, end)
        accumulate(2, f)
    for f in fields:
        relay_x(1, f, late)
        accumulate(3, f)
    for f in fields:
        accumulate(1, f)
    fixed.wait_recv()
    fixed.wait_send()

    full = rows + HALO
    line = lax.broadcasted_iota(jnp.int32, (full, 256), 0)
    above = jnp.where((line == 0) & (y == 0), 0.0, 1.0)
    below = jnp.where((line == rows - 1) & (y == 1), 0.0, 1.0)

    def dx(a):
        return pltpu.roll(a, full - 1, 0) * below - pltpu.roll(a, 1, 0) * above

    def dy(a):
        return pltpu.roll(a, a.shape[1] - 1, 1) - pltpu.roll(a, 1, 1)

    plane[0] = -SIGMA * plane[0]
    h, u, v = z_acc[SWEEPS, 0], z_acc[SWEEPS, 1], z_acc[SWEEPS, 2]
    for n in reversed(range(SWEEPS)):
        scaled_depth, turn = plane[0], plane[1]
        h, u, v = (
            z_acc[n, 0] + scaled_depth * (dx(u) + dy(v)),
            z_acc[n, 1] - SIGMA * dx(h) + turn * v,
            z_acc[n, 2] - SIGMA * dy(h) - turn * u,
        )
    out[0, 0] = h[:rows]
    out[0, 1] = u[:rows]
    out[0, 2] = v[:rows]

    for finish in pending:
        finish()
    edges.wait_send()


def shards_kernel(rhs, depth, coriolis):
    window = lax.axis_size("tm")
    _, fields, rows, columns = rhs.shape
    far = pl.BlockSpec(memory_space=pltpu.HBM)
    dma = pltpu.SemaphoreType.DMA
    return pl.pallas_call(
        functools.partial(gather_kernel, window, rows, coefficients(window)),
        out_shape=jax.ShapeDtypeStruct(rhs.shape, jnp.float32),
        in_specs=[far, far, far],
        out_specs=pl.BlockSpec(memory_space=pltpu.VMEM),
        scratch_shapes=[
            pltpu.VMEM((window, fields, rows + HALO, columns), jnp.float32),
            pltpu.VMEM((2, rows + HALO, columns), jnp.float32),
            pltpu.VMEM((TERMS, fields, rows + HALO, columns), jnp.float32),
            pltpu.SMEM((TERMS, 2 * window - 1), jnp.float32),
            dma((48,)), dma((6, 4)), dma((window, fields)), dma((3,)), dma((2,)), dma((2,)),
        ],
        compiler_params=pltpu.CompilerParams(collective_id=0, has_side_effects=True, vmem_limit_bytes=62 << 20),
        cost_estimate=pl.CostEstimate(flops=40_000_000, bytes_accessed=1_000_000, transcendentals=0),
    )(rhs, depth, coriolis)


def shards_plain(rhs, depth, coriolis):
    window, tiles = lax.axis_size("tm"), lax.axis_size("space")
    tm = lax.axis_index("tm")

    def widen(a, dim):
        length = a.shape[dim]
        last = lax.slice_in_dim(a, length - HALO, length, axis=dim)
        first = lax.slice_in_dim(a, 0, HALO, axis=dim)
        before = lax.ppermute(last, "space", [(i, i + 1) for i in range(tiles - 1)])
        after = lax.ppermute(first, "space", [(i + 1, i) for i in range(tiles - 1)])
        return jnp.concatenate([before, a, after], axis=dim)

    table = jnp.asarray(coefficients(window))
    mine = lax.dynamic_slice_in_dim(table, tm, window, axis=1)[:, ::-1]
    wide = widen(rhs[0], 1)
    everyone = lax.all_gather(wide, "tm")
    sums = jnp.einsum("nj,jfxy->nfxy", mine, everyone, precision=lax.Precision.HIGHEST)
    rows = rhs.shape[2]
    line = lax.axis_index("space") * rows - HALO + jnp.arange(rows + 2 * HALO)
    inside = ((line >= 0) & (line < rows * tiles)).astype(jnp.float32)[:, None]
    deep, turn = -SIGMA * widen(depth, 0), widen(coriolis, 0)

    def dx(a):
        return (jnp.roll(a, -1, 0) - jnp.roll(a, 1, 0)) * inside

    def dy(a):
        return jnp.roll(a, -1, 1) - jnp.roll(a, 1, 1)

    h, u, v = sums[SWEEPS]
    for n in reversed(range(SWEEPS)):
        h, u, v = (sums[n, 0] + deep * (dx(u) + dy(v)), sums[n, 1] - SIGMA * dx(h) + turn * v,
                   sums[n, 2] - SIGMA * dy(h) - turn * u)
    return jnp.stack([h, u, v])[None, :, HALO:rows + HALO]


def solution(mesh):
    in_specs = (P("tm", None, "space", None), P("space", None), P("space", None))
    out_specs = P("tm", None, "space", None)
    body = shards_kernel if (mesh.shape["tm"], mesh.shape["space"]) == (16, 2) else shards_plain
    return jax.shard_map(body, mesh=mesh, in_specs=in_specs, out_specs=out_specs, check_vma=False)
```

```python
import functools

import jax
import jax.numpy as jnp
import numpy as np
from jax import lax
from jax.experimental import pallas as pl
from jax.experimental.pallas import tpu as pltpu
from jax.sharding import PartitionSpec as P

SWEEPS = 8
RHO = 0.9
SIGMA = 0.01
TERMS = SWEEPS + 1
CHUNKS = 4
HALO = 8
MESH = pl.DeviceIdType.MESH


def coefficients(window):
    k = np.arange(window)
    lam = 1.0 - RHO * np.exp(-2j * np.pi * k / window)
    gap = np.arange(-(window - 1), window)
    phase = np.exp(2j * np.pi * gap[:, None] * k[None, :] / window)
    powers = np.stack([lam ** -(n + 1.0) for n in range(TERMS)])
    table = (powers @ phase.T).real / window * RHO ** (-gap.astype(np.float64))
    return table.astype(np.float32)


def gather_kernel(window, rows, table, rhs, depth, coriolis, out, main, plane, z_acc, coef, send_sem, recv_sem,
                  local_sem, send_y, recv_y):
    tm, y = lax.axis_index("tm"), lax.axis_index("space")
    z, x, c = tm // 4, tm % 4 // 2, tm % 2
    end = (z == 0) | (z == 3)
    inner = jnp.logical_not(end)
    groups = (rows + HALO) // HALO
    cuts = [groups * q // CHUNKS * HALO for q in range(CHUNKS + 1)]
    chunks = [(lo, hi - lo) for lo, hi in zip(cuts, cuts[1:])]
    parts_of = range(CHUNKS)
    pair = z + 1 - 2 * (z % 2)
    order = [z, pair, jnp.where(z < 2, 2, 1), jnp.where(z < 2, 3, 0)]
    x_other, c_other = z * 4 + (1 - x) * 2 + c, z * 4 + x * 2 + 1 - c

    loads = [
        pltpu.make_async_copy(rhs.at[0], main.at[tm, :, pl.ds(0, rows), :], local_sem.at[0]),
        pltpu.make_async_copy(depth, plane.at[0, pl.ds(0, rows), :], local_sem.at[1]),
        pltpu.make_async_copy(coriolis, plane.at[1, pl.ds(0, rows), :], local_sem.at[2]),
    ]
    for load in loads:
        load.start()

    barrier = pltpu.get_barrier_semaphore()
    for peer in (x_other, c_other):
        pl.semaphore_signal(barrier, inc=1, device_id={"tm": peer}, device_id_type=MESH)
    pl.semaphore_signal(barrier, inc=1, device_id={"space": 1 - y}, device_id_type=MESH)

    for hop in (-4, 4):
        there = tm + hop

        @pl.when((there >= 0) & (there < window))
        def _():
            pl.semaphore_signal(barrier, inc=1, device_id={"tm": there}, device_id_type=MESH)

    for n in range(TERMS):
        for gap in range(2 * window - 1):
            coef[n, gap] = float(table[n, gap])
    for load in loads:
        load.wait()
    pl.semaphore_wait(barrier, jnp.where(end, 4, 5))

    both = lambda *conds: functools.reduce(jnp.logical_and, conds) if conds else None

    def guarded(when, act):
        if when is None:
            act()
        else:
            pl.when(when)(act)

    def copy(block, q, slot, peer):
        ref = main.at[block, :, pl.ds(*chunks[q]), :]
        return pltpu.make_async_remote_copy(
            src_ref=ref, dst_ref=ref, send_sem=send_sem.at[slot], recv_sem=recv_sem.at[block, q],
            device_id={"tm": peer}, device_id_type=MESH)

    always, when_inner, when_cross, when_second = range(4)

    def send(kind, block, q, peer, start_when=None):
        guarded(start_when, lambda: copy(block, q, kind, peer).start())

    def all_sent(kind, blocks, when=None):
        ref = main.at[pl.ds(0, blocks)]
        sent = pltpu.make_async_remote_copy(
            src_ref=ref, dst_ref=ref, send_sem=send_sem.at[kind], recv_sem=recv_sem.at[0, 0],
            device_id={"tm": c_other}, device_id_type=MESH)
        guarded(when, sent.wait_send)

    def arrived(block, f):
        copy(block, f, 0, c_other).wait_recv()

    def block_of(stage, same_x, same_c):
        return order[stage] * 4 + (x if same_x else 1 - x) * 2 + (c if same_c else 1 - c)

    edge = pl.multiple_of((1 - y) * (rows - HALO), HALO)
    tail = pl.ds(rows, HALO)
    edges = pltpu.make_async_remote_copy(
        src_ref=main.at[tm, :, pl.ds(edge, HALO), :], dst_ref=main.at[tm, :, tail, :], send_sem=send_y.at[0],
        recv_sem=recv_y.at[0], device_id={"space": 1 - y}, device_id_type=MESH)
    fixed = pltpu.make_async_remote_copy(
        src_ref=plane.at[:, pl.ds(edge, HALO), :], dst_ref=plane.at[:, tail, :], send_sem=send_y.at[1],
        recv_sem=recv_y.at[1], device_id={"space": 1 - y}, device_id_type=MESH)
    edges.start()

    def own(q):
        outward = jnp.where(z < 2, 4, -4)
        send(always, tm, q, tm + outward)
        send(always, tm, q, x_other)
        send(when_inner, tm, q, tm - outward, inner)
        send(always, tm, q, c_other)

    def relay_z(stage, q, when=None):
        block = block_of(stage, True, True)
        guarded(when, lambda: arrived(block, q))
        conds = [] if when is None else [when]
        onward = jnp.where(order[stage] < z, z + 1, z - 1)
        send(when_inner, block, q, onward * 4 + x * 2 + c, both(inner, *conds))
        cross = [end & (c == 1)] if stage == 1 else []
        send(when_cross if cross else always, block, q, x_other, both(*cross, *conds))
        send(always, block, q, c_other, both(*conds))

    def relay_x(stage, q, when=None):
        block = block_of(stage, False, True)
        guarded(when, lambda: arrived(block, q))
        send(always, block, q, c_other, when)

    def second_route(q, when):
        send(when_second, block_of(0, False, True), q, pair * 4 + x * 2 + c, when)

    def accumulate(stage, q, first=False):
        arrived(block_of(stage, True, False), q)
        arrived(block_of(stage, False, False), q)
        blocks = [order[stage] * 4 + k for k in range(4)]
        weights = [[coef[n, tm - b + window - 1] for b in blocks] for n in range(TERMS)]
        part = pl.ds(*chunks[q])

        def body(f, carry):
            parts = [main[b, f, part] for b in blocks]
            for n in range(TERMS):
                total = parts[0] * weights[n][0]
                for k in range(1, 4):
                    total = total + parts[k] * weights[n][k]
                if not first:
                    total = total + z_acc[n, f, part]
                z_acc[n, f, part] = total
            return carry

        lax.fori_loop(0, 3, body, 0)

    for q in parts_of[:-1]:
        own(q)
    edges.wait_recv()
    own(CHUNKS - 1)
    fixed.start()

    late = end & (c == 0)
    for q in parts_of:
        relay_z(1, q)
        relay_z(2, q, inner)
        relay_x(0, q)
        second_route(q, end)
    for q in parts_of:
        relay_z(3, q, inner)
        relay_z(2, q, end)
        relay_x(1, q, jnp.logical_not(late))
        relay_x(2, q, inner)
        accumulate(0, q, True)
    for q in parts_of:
        second_route(q, inner & (c == 0))
    for q in parts_of:
        relay_z(3, q, end)
        relay_x(2, q, end)
        relay_x(3, q, inner)
    for q in parts_of:
        relay_x(3, q, end)
        accumulate(2, q)
    for q in parts_of:
        relay_x(1, q, late)
        accumulate(3, q)
    for q in parts_of:
        accumulate(1, q)
    fixed.wait_recv()
    fixed.wait_send()

    full = rows + HALO
    line = lax.broadcasted_iota(jnp.int32, (full, 256), 0)
    above = jnp.where((line == 0) & (y == 0), 0.0, 1.0)
    below = jnp.where((line == rows - 1) & (y == 1), 0.0, 1.0)

    def dx(a):
        return pltpu.roll(a, full - 1, 0) * below - pltpu.roll(a, 1, 0) * above

    def dy(a):
        return pltpu.roll(a, a.shape[1] - 1, 1) - pltpu.roll(a, 1, 1)

    plane[0] = -SIGMA * plane[0]
    h, u, v = z_acc[SWEEPS, 0], z_acc[SWEEPS, 1], z_acc[SWEEPS, 2]
    for n in reversed(range(SWEEPS)):
        scaled_depth, turn = plane[0], plane[1]
        h, u, v = (
            z_acc[n, 0] + scaled_depth * (dx(u) + dy(v)),
            z_acc[n, 1] - SIGMA * dx(h) + turn * v,
            z_acc[n, 2] - SIGMA * dy(h) - turn * u,
        )
    out[0, 0] = h[:rows]
    out[0, 1] = u[:rows]
    out[0, 2] = v[:rows]

    all_sent(always, 12)
    all_sent(when_inner, 4, inner)
    all_sent(when_cross, 1, end & (c == 1))
    all_sent(when_second, 1, end | (c == 0))
    edges.wait_send()


def shards_kernel(rhs, depth, coriolis):
    window = lax.axis_size("tm")
    _, fields, rows, columns = rhs.shape
    far = pl.BlockSpec(memory_space=pltpu.HBM)
    dma = pltpu.SemaphoreType.DMA
    return pl.pallas_call(
        functools.partial(gather_kernel, window, rows, coefficients(window)),
        out_shape=jax.ShapeDtypeStruct(rhs.shape, jnp.float32),
        in_specs=[far, far, far],
        out_specs=pl.BlockSpec(memory_space=pltpu.VMEM),
        scratch_shapes=[
            pltpu.VMEM((window, fields, rows + HALO, columns), jnp.float32),
            pltpu.VMEM((2, rows + HALO, columns), jnp.float32),
            pltpu.VMEM((TERMS, fields, rows + HALO, columns), jnp.float32),
            pltpu.SMEM((TERMS, 2 * window - 1), jnp.float32),
            dma((4,)), dma((window, CHUNKS)), dma((3,)), dma((2,)), dma((2,)),
        ],
        compiler_params=pltpu.CompilerParams(collective_id=0, has_side_effects=True, vmem_limit_bytes=62 << 20),
        cost_estimate=pl.CostEstimate(flops=40_000_000, bytes_accessed=1_000_000, transcendentals=0),
    )(rhs, depth, coriolis)


def shards_plain(rhs, depth, coriolis):
    window, tiles = lax.axis_size("tm"), lax.axis_size("space")
    tm = lax.axis_index("tm")

    def widen(a, dim):
        length = a.shape[dim]
        last = lax.slice_in_dim(a, length - HALO, length, axis=dim)
        first = lax.slice_in_dim(a, 0, HALO, axis=dim)
        before = lax.ppermute(last, "space", [(i, i + 1) for i in range(tiles - 1)])
        after = lax.ppermute(first, "space", [(i + 1, i) for i in range(tiles - 1)])
        return jnp.concatenate([before, a, after], axis=dim)

    table = jnp.asarray(coefficients(window))
    mine = lax.dynamic_slice_in_dim(table, tm, window, axis=1)[:, ::-1]
    wide = widen(rhs[0], 1)
    everyone = lax.all_gather(wide, "tm")
    sums = jnp.einsum("nj,jfxy->nfxy", mine, everyone, precision=lax.Precision.HIGHEST)
    rows = rhs.shape[2]
    line = lax.axis_index("space") * rows - HALO + jnp.arange(rows + 2 * HALO)
    inside = ((line >= 0) & (line < rows * tiles)).astype(jnp.float32)[:, None]
    deep, turn = -SIGMA * widen(depth, 0), widen(coriolis, 0)

    def dx(a):
        return (jnp.roll(a, -1, 0) - jnp.roll(a, 1, 0)) * inside

    def dy(a):
        return jnp.roll(a, -1, 1) - jnp.roll(a, 1, 1)

    h, u, v = sums[SWEEPS]
    for n in reversed(range(SWEEPS)):
        h, u, v = (sums[n, 0] + deep * (dx(u) + dy(v)), sums[n, 1] - SIGMA * dx(h) + turn * v,
                   sums[n, 2] - SIGMA * dy(h) - turn * u)
    return jnp.stack([h, u, v])[None, :, HALO:rows + HALO]


def solution(mesh):
    in_specs = (P("tm", None, "space", None), P("space", None), P("space", None))
    out_specs = P("tm", None, "space", None)
    body = shards_kernel if (mesh.shape["tm"], mesh.shape["space"]) == (16, 2) else shards_plain
    return jax.shard_map(body, mesh=mesh, in_specs=in_specs, out_specs=out_specs, check_vma=False)
```
